256 devices in a mesh: ep: 32 (over z, y), dp: 8 (over x, core).
Axes of the slice: x: 4, y: 4, z: 8, core: 2. Of those that a mesh axis runs over, the one named last changes fastest.
Arguments:
- hidden_rows: bfloat16 [64, 1792, 1024], P('ep', None, 'dp'), may hold values from -6 to 6
- out_grad: bfloat16 [64, 1792, 3584], P('ep', None, 'dp'), may hold values from -0.75 to 0.75
- row_counts: int32 [64], P('ep'), may hold values from 1 to 1792, as said below
- replicas: int32 [32, 8], replicated, may hold values from -1 to 63, as said below
- next_replicas: int32 [32, 8], replicated, may hold values from -1 to 63, as said below
- owner_map: int32 [32], replicated, may hold values from 0 to 31, each once
- master: float32 [32, 3584, 1024], P('ep', 'dp'), may hold values from -0.1875 to 0.1875
- first_moment: bfloat16 [32, 3584, 1024], P('ep', 'dp'), may hold values from -3 to 3
- second_moment: bfloat16 [32, 3584, 1024], P('ep', 'dp'), may hold values from 0.0099487305 to 1
Outputs:
- new_master: float32 [32, 3584, 1024], P('ep', 'dp')
- new_first_moment: bfloat16 [32, 3584, 1024], P('ep', 'dp')
- new_second_moment: bfloat16 [32, 3584, 1024], P('ep', 'dp')
- next_copies: bfloat16 [64, 3584, 1024], P('ep', 'dp')
The draws below stay inside these ranges and needn't reach their ends.
Inputs may be any that keep to these rules, and one draw needn't show every extreme that they name: Rows of slot g past row_counts[g] are unused; some slot is full in every draw. `replicas`: each of the 64 slots appears in exactly one list; a list holds its slots first and -1 after them; every expert has 1 to 8 copies and some expert has exactly 8. `next_replicas`: same form as replicas. `owner_map`: each ep index owns exactly one expert.
All inputs are finite; a program needn't handle non-finite values.
Results may differ from the reference program's by a relative error of at most 0.017.
Values may be sent and summed in bfloat16 or wider, within the bound.
No kernel may reach another device: no remote copies, remote signals or barrier semaphores. Data moves between devices by JAX's collectives and lax.ppermute only.
A program may use at most 64 MiB of HBM per device.

```python
import math
import jax
import jax.numpy as jnp
from jax import lax

D = 3584
FF = 1024
SLOTS = 2
CMAX = 8
ROWS = 1792
EXPERTS = 32
COPIES = 64


def copy_lists(base_key, total_slots, experts, most_copies):
    hot_key, pick_key, perm_key = jax.random.split(base_key, 3)
    hot_expert = jax.random.randint(hot_key, (), 0, experts)
    expert_ids = jnp.arange(experts, dtype=jnp.int32)
    tallies = jnp.where(expert_ids == hot_expert, most_copies, 1).astype(jnp.int32)
    extra_slots = total_slots - most_copies - (experts - 1)

    def add_one(turn_index, current_tallies):
        open_weight = jnp.where((current_tallies < most_copies) & (expert_ids != hot_expert), current_tallies, 0)
        weight_sum = jnp.sum(open_weight)
        pick_value = jax.random.randint(jax.random.fold_in(pick_key, turn_index), (), 0, weight_sum)
        chosen = jnp.sum((jnp.cumsum(open_weight) <= pick_value).astype(jnp.int32))
        return current_tallies + (expert_ids == chosen).astype(jnp.int32)
    tallies = lax.fori_loop(0, extra_slots, add_one, tallies)
    slot_order = jax.random.permutation(perm_key, total_slots).astype(jnp.int32)
    start_at = jnp.cumsum(tallies) - tallies
    column_ids = jnp.arange(most_copies, dtype=jnp.int32)
    positions = start_at[:, None] + column_ids[None, :]
    taken_slots = slot_order[jnp.clip(positions, 0, total_slots - 1)]
    return jnp.where(column_ids[None, :] < tallies[:, None], taken_slots, -1).astype(jnp.int32)


def draw_replicas(key, part):
    key = jax.random.fold_in(key, 11)
    return copy_lists(key, EXPERTS * SLOTS, EXPERTS, CMAX)


def draw_next_replicas(key, part):
    key = jax.random.fold_in(key, 12)
    return copy_lists(key, EXPERTS * SLOTS, EXPERTS, CMAX)


def draw_row_counts(key, part):
    key = jax.random.fold_in(key, 13)
    count_key, full_key = jax.random.split(key)
    tallies = jax.random.randint(count_key, (EXPERTS * SLOTS,), 1, ROWS + 1)
    full_slot = jax.random.randint(full_key, (), 0, EXPERTS * SLOTS)
    slot_ids = jnp.arange(EXPERTS * SLOTS, dtype=jnp.int32)
    return jnp.where(slot_ids == full_slot, ROWS, tallies).astype(jnp.int32)


def level_of(rng, dims, pieces, low, largest):
    level = 1.0
    for axis_at, parts in pieces:
        heights = jax.random.uniform(jax.random.fold_in(jax.random.fold_in(rng, 6), axis_at), (parts,), jnp.float32, low / len(pieces), largest / len(pieces))
        level = level * jnp.repeat(jnp.exp(heights), dims[axis_at] // parts).reshape((-1,) + (1,) * (len(dims) - 1 - axis_at))
    return level


def scatter_about(key, extent, spread, limit, cuts=(), kind=jnp.bfloat16):
    entries = jax.random.normal(key, extent, jnp.float32) * spread
    if len(cuts) > 0:
        entries = level_of(key, extent, cuts, -0.22, 0.18) * entries
    return jnp.clip(entries, min=-limit, max=limit).astype(kind)


def setup_inputs(seed: int = 0) -> dict:
    key_of = jax.random.split(jax.random.key(seed), 10)
    hidden_rows = scatter_about(key_of[0], (COPIES, ROWS, FF), 1.0, 6.0, ((0, 32), (2, 8)))
    out_grad = scatter_about(key_of[1], (COPIES, ROWS, D), 0.05, 0.75, ((0, 32), (2, 8)))
    row_counts = draw_row_counts(jax.random.fold_in(key_of[9], 71), 0)
    replicas = draw_replicas(jax.random.fold_in(key_of[9], 71), 0)
    next_replicas = draw_next_replicas(jax.random.fold_in(key_of[9], 71), 0)
    owner_map = jax.random.permutation(key_of[5], EXPERTS).astype(jnp.int32)
    master = scatter_about(key_of[6], (EXPERTS, D, FF), FF ** -0.5, 0.1875, ((0, 32), (1, 8)), jnp.float32)
    first_moment = scatter_about(key_of[7], (EXPERTS, D, FF), 0.3, 3.0, ((0, 32), (1, 8)))
    second_moment = jnp.clip(jnp.exp(math.log(1.0) - 4.61031033 * jax.random.uniform(key_of[8], (EXPERTS, D, FF), jnp.float32) ** level_of(key_of[8], (EXPERTS, D, FF), ((0, 32), (1, 8)), -0.2, 0.2)), 0.0099487305, 1.0).astype(jnp.bfloat16)
    return {"hidden_rows": hidden_rows, "out_grad": out_grad, "row_counts": row_counts, "replicas": replicas, "next_replicas": next_replicas, "owner_map": owner_map, "master": master, "first_moment": first_moment, "second_moment": second_moment}


beta_first = 0.9
beta_second = 0.95
learn_rate = 0.001
adam_epsilon = 1e-08

def holder_experts(replicas, total_slots):
    slot_ids = jnp.arange(total_slots, dtype=jnp.int32)
    hold_table = jnp.any(replicas[:, :, None] == slot_ids[None, None, :], axis=1).astype(jnp.int32)
    expert_ids = jnp.arange(replicas.shape[0], dtype=jnp.int32)
    return lax.optimization_barrier(jnp.sum(hold_table * expert_ids[:, None], axis=0))

def slot_owners(replicas, owner_map, total_slots):
    experts = holder_experts(replicas, total_slots)
    picked = experts[:, None] == jnp.arange(owner_map.shape[0], dtype=jnp.int32)[None, :]
    return lax.optimization_barrier(jnp.sum(jnp.where(picked, owner_map[None, :], 0), axis=1)).astype(jnp.int32)

def reference(hidden_rows, out_grad, row_counts, replicas, next_replicas, owner_map, master, first_moment, second_moment):
    total_slots = hidden_rows.shape[0]
    row_total = hidden_rows.shape[1]
    owners_now = slot_owners(replicas, owner_map, total_slots)
    owners_next = slot_owners(next_replicas, owner_map, total_slots)
    row_ids = jnp.arange(row_total, dtype=jnp.int32)

    def add_slot(totals, inputs):
        hidden_slot, grad_slot, count_slot, owner_slot = inputs
        masked = jnp.where((row_ids < count_slot)[:, None], grad_slot, jnp.zeros_like(grad_slot))
        product = lax.dot_general(masked, hidden_slot, (((0,), (0,)), ((), ())), preferred_element_type=jnp.float32)
        current = lax.dynamic_index_in_dim(totals, owner_slot, 0, keepdims=False)
        totals = lax.dynamic_update_index_in_dim(totals, current + product, owner_slot, 0)
        return (totals, None)
    start_totals = jnp.zeros(master.shape, jnp.float32)
    gradient, unused = lax.scan(add_slot, start_totals, (hidden_rows, out_grad, row_counts, owners_now))
    first_new = beta_first * first_moment.astype(jnp.float32) + (1.0 - beta_first) * gradient
    second_new = beta_second * second_moment.astype(jnp.float32) + (1.0 - beta_second) * gradient * gradient
    updated = master - learn_rate * first_new / (jnp.sqrt(second_new) + adam_epsilon)
    copies = jnp.take(updated.astype(jnp.bfloat16), owners_next, axis=0)
    return (updated, first_new.astype(jnp.bfloat16), second_new.astype(jnp.bfloat16), copies)
```

```python
import functools

import jax
import jax.numpy as jnp
from jax import lax
from jax.experimental import pallas as pl
from jax.experimental.pallas import tpu as pltpu
from jax.sharding import PartitionSpec as P

beta_first = 0.9
beta_second = 0.95
learn_rate = 0.001
adam_epsilon = 1e-08

ROW_CUTS = 4
COL_CUTS = 8
PIECE = 112
LANES = 128
VMEM = 48 * 1024 * 1024


def any_spec():
    return pl.BlockSpec(memory_space=pl.ANY)


def smem_spec():
    return pl.BlockSpec(memory_space=pltpu.SMEM)


def grad_kernel(slot, place_ref, counts_ref, grad_ref, *refs):
    shard_refs = refs[:8]
    out_ref, grad_v, hidden_v, grad_sem, hidden_sems = refs[8:]
    shards_x = COL_CUTS // 2
    load_grad = pltpu.make_async_copy(grad_ref.at[slot], grad_v, grad_sem)
    load_grad.start()
    loads = []
    for j in range(shards_x):
        for c in range(2):
            src = shard_refs[2 * j + c]
            if len(src.shape) == 3:
                src = src.at[slot]
            load = pltpu.make_async_copy(
                src, hidden_v.at[j, :, pl.ds(c * LANES, LANES)], hidden_sems.at[j, c]
            )
            load.start()
            loads.append(load)
    load_grad.wait()
    count = counts_ref[slot]
    rows = grad_v.shape[1]
    live = lax.broadcasted_iota(jnp.int32, (PIECE, rows), 1) < count
    for r in range(ROW_CUTS):
        cut = grad_v[pl.ds(r * PIECE, PIECE), :]
        grad_v[pl.ds(r * PIECE, PIECE), :] = jnp.where(live, cut, jnp.zeros_like(cut))
    for load in loads:
        load.wait()
    x_here = place_ref[0] // 2
    core_here = lax.rem(place_ref[0], 2)

    @pl.loop(0, shards_x)
    def _(j):
        product = jnp.dot(grad_v[...], hidden_v[j], preferred_element_type=jnp.float32)
        product = product.astype(out_ref.dtype)
        x_there = lax.rem(x_here + j, shards_x)
        for c in range(2):
            column = 2 * x_there + (core_here if c == 0 else 1 - core_here)
            for r in range(ROW_CUTS):
                out_ref[r * COL_CUTS + column] = product[
                    r * PIECE : (r + 1) * PIECE, c * LANES : (c + 1) * LANES
                ]


def slot_gradient(slot, place, counts, grad_t, shards):
    rows = grad_t.shape[2]
    width = grad_t.shape[1]
    return pl.pallas_call(
        functools.partial(grad_kernel, slot),
        out_shape=jax.ShapeDtypeStruct((ROW_CUTS * COL_CUTS, PIECE, LANES), jnp.bfloat16),
        in_specs=[smem_spec(), smem_spec()] + [any_spec()] * 9,
        out_specs=pl.BlockSpec(memory_space=pltpu.VMEM),
        scratch_shapes=[
            pltpu.VMEM((width, rows), jnp.bfloat16),
            pltpu.VMEM((COL_CUTS // 2, rows, 2 * LANES), jnp.bfloat16),
            pltpu.SemaphoreType.DMA,
            pltpu.SemaphoreType.DMA((COL_CUTS // 2, 2)),
        ],
        compiler_params=pltpu.CompilerParams(vmem_limit_bytes=VMEM),
        cost_estimate=pl.CostEstimate(
            flops=2 * width * rows * 1024, bytes_accessed=8_000_000, transcendentals=0
        ),
        name="slot_gradient",
    )(place, counts, grad_t, *shards)


def list_length(lists_ref, e):
    length = jnp.int32(0)
    for j in range(lists_ref.shape[1]):
        length = length + (lists_ref[e, j] >= 0).astype(jnp.int32)
    return length


def sum_kernel(replicas_ref, owners_ref, first_ref, second_ref, out_ref, held, sems):
    loads = [
        pltpu.make_async_copy(src, held.at[s], sems.at[s])
        for s, src in enumerate((first_ref, second_ref))
    ]
    for load in loads:
        load.start()
    for load in loads:
        load.wait()

    @pl.loop(0, replicas_ref.shape[0])
    def _(e):
        def add(j, total):
            g = replicas_ref[e, j]
            return total + held[lax.rem(g, 2), g // 2].astype(jnp.float32)

        total = lax.fori_loop(
            0, list_length(replicas_ref, e), add, jnp.zeros((PIECE, LANES), jnp.float32)
        )
        out_ref[owners_ref[e]] = total.astype(out_ref.dtype)


def sum_copies(replicas, owner_map, first, second):
    pieces = first.shape[0]
    return pl.pallas_call(
        sum_kernel,
        out_shape=jax.ShapeDtypeStruct((pieces, PIECE, LANES), jnp.bfloat16),
        in_specs=[smem_spec(), smem_spec(), any_spec(), any_spec()],
        out_specs=pl.BlockSpec(memory_space=pltpu.VMEM),
        scratch_shapes=[
            pltpu.VMEM((2, pieces, PIECE, LANES), jnp.bfloat16),
            pltpu.SemaphoreType.DMA((2,)),
        ],
        compiler_params=pltpu.CompilerParams(vmem_limit_bytes=VMEM),
        name="sum_copies",
    )(replicas, owner_map, first, second)


def adam_kernel(grad_ref, master_ref, first_ref, second_ref, master_out, first_out, second_out, sent_ref):
    for c in range(COL_CUTS):
        cut = pl.ds(c * LANES, LANES)
        gradient = grad_ref[c].astype(jnp.float32)
        first_new = beta_first * first_ref[0, :, cut].astype(jnp.float32) + (1.0 - beta_first) * gradient
        second_new = (
            beta_second * second_ref[0, :, cut].astype(jnp.float32)
            + (1.0 - beta_second) * gradient * gradient
        )
        updated = master_ref[0, :, cut] - learn_rate * first_new / (jnp.sqrt(second_new) + adam_epsilon)
        master_out[0, :, cut] = updated
        first_out[0, :, cut] = first_new.astype(first_out.dtype)
        second_out[0, :, cut] = second_new.astype(second_out.dtype)
        sent_ref[c] = updated.astype(sent_ref.dtype)


def adam_update(gradient, master, first_moment, second_moment):
    rows = pl.BlockSpec((1, PIECE, COL_CUTS * LANES), lambda r: (0, r, 0))
    pieces = pl.BlockSpec((COL_CUTS, PIECE, LANES), lambda r: (r, 0, 0))
    return pl.pallas_call(
        adam_kernel,
        grid=(ROW_CUTS,),
        out_shape=(
            jax.ShapeDtypeStruct(master.shape, jnp.float32),
            jax.ShapeDtypeStruct(master.shape, jnp.bfloat16),
            jax.ShapeDtypeStruct(master.shape, jnp.bfloat16),
            jax.ShapeDtypeStruct(gradient.shape, jnp.bfloat16),
        ),
        in_specs=[pieces, rows, rows, rows],
        out_specs=(rows, rows, rows, pieces),
        compiler_params=pltpu.CompilerParams(vmem_limit_bytes=VMEM),
        name="adam_update",
    )(gradient, master, first_moment, second_moment)


def spread_kernel(lists_ref, owners_ref, weights_ref, out_ref):
    @pl.loop(0, lists_ref.shape[0])
    def _(e):
        weights = weights_ref[owners_ref[e]]

        def put(j, carry):
            g = lists_ref[e, j]
            out_ref[g // 2, lax.rem(g, 2)] = weights
            return carry

        lax.fori_loop(0, list_length(lists_ref, e), put, 0)


def spread_copies(next_replicas, owner_map, weights):
    pieces = weights.shape[0]
    return pl.pallas_call(
        spread_kernel,
        out_shape=jax.ShapeDtypeStruct((pieces, 2, PIECE, LANES), jnp.bfloat16),
        in_specs=[smem_spec(), smem_spec(), pl.BlockSpec(memory_space=pltpu.VMEM)],
        out_specs=pl.BlockSpec(memory_space=pltpu.VMEM),
        compiler_params=pltpu.CompilerParams(vmem_limit_bytes=VMEM),
        name="spread_copies",
    )(next_replicas, owner_map, weights)


def order_kernel(pieces_ref, out_ref):
    for c in range(COL_CUTS):
        out_ref[0, :, pl.ds(c * LANES, LANES)] = pieces_ref[c, 0]


def order_pieces(pieces):
    width = ROW_CUTS * PIECE
    return pl.pallas_call(
        order_kernel,
        grid=(2, ROW_CUTS),
        out_shape=jax.ShapeDtypeStruct((2, width, COL_CUTS * LANES), jnp.bfloat16),
        in_specs=[pl.BlockSpec((COL_CUTS, 1, PIECE, LANES), lambda s, r: (r, s, 0, 0))],
        out_specs=pl.BlockSpec((1, PIECE, COL_CUTS * LANES), lambda s, r: (s, r, 0)),
        compiler_params=pltpu.CompilerParams(vmem_limit_bytes=VMEM),
        name="order_pieces",
    )(pieces)


def x_shift(array, step):
    pairs = [(2 * x + c, 2 * ((x + step) % 4) + c) for x in range(4) for c in range(2)]
    return lax.ppermute(array, "dp", pairs)


def core_swap(array):
    pairs = [(2 * x + c, 2 * x + 1 - c) for x in range(4) for c in range(2)]
    return lax.ppermute(array, "dp", pairs)


def gather_hidden(own):
    ahead = x_shift(own, -1)
    behind = x_shift(own, 1)
    across = x_shift(own, 2)
    mine = [own, ahead, across, behind]
    return [shard for pair in zip(mine, [core_swap(shard) for shard in mine]) for shard in pair]


def exchange(pieces):
    return lax.all_to_all(pieces, "ep", split_axis=0, concat_axis=0, tiled=True)


def shards(
    hidden_rows,
    out_grad,
    row_counts,
    replicas,
    next_replicas,
    owner_map,
    master,
    first_moment,
    second_moment,
):
    place = lax.axis_index("dp").reshape(1).astype(jnp.int32)
    grad_t = jnp.swapaxes(out_grad, 1, 2)
    hidden_first = gather_hidden(hidden_rows[0])
    later, *hidden_first = lax.optimization_barrier((hidden_rows[1], *hidden_first))
    hidden_second = gather_hidden(later)
    received_first = exchange(slot_gradient(0, place, row_counts, grad_t, hidden_first))
    received_second = exchange(slot_gradient(1, place, row_counts, grad_t, hidden_second))
    owner_pieces = sum_copies(replicas, owner_map, received_first, received_second)
    gradient = exchange(owner_pieces)
    updated, new_first, new_second, weight_pieces = adam_update(
        gradient, master, first_moment, second_moment
    )
    copies = spread_copies(next_replicas, owner_map, exchange(weight_pieces))
    next_copies = order_pieces(exchange(copies))
    return (updated, new_first, new_second, next_copies)


def solution(mesh):
    placed = (
        P("ep", None, "dp"),
        P("ep", None, "dp"),
        P("ep"),
        P(),
        P(),
        P(),
        P("ep", "dp", None),
        P("ep", "dp", None),
        P("ep", "dp", None),
    )
    return jax.shard_map(
        shards,
        mesh=mesh,
        in_specs=placed,
        out_specs=(
            P("ep", "dp", None),
            P("ep", "dp", None),
            P("ep", "dp", None),
            P("ep", "dp", None),
        ),
        check_vma=False,
    )
```

```python
import functools

import jax
import jax.numpy as jnp
from jax import lax
from jax.experimental import pallas as pl
from jax.experimental.pallas import tpu as pltpu
from jax.sharding import PartitionSpec as P

beta_first = 0.9
beta_second = 0.95
learn_rate = 0.001
adam_epsilon = 1e-08

ROW_CUTS = 4
COL_CUTS = 8
PIECE = 112
LANES = 128
VMEM = 48 * 1024 * 1024
VMEM_FAR = 48 * 1024 * 1024
VMEM_ALL = 62 * 1024 * 1024


def any_spec():
    return pl.BlockSpec(memory_space=pl.ANY)


def smem_spec():
    return pl.BlockSpec(memory_space=pltpu.SMEM)


def grad_kernel(slot, columns, place_ref, counts_ref, grad_ref, *refs):
    taken = sum(len(parts) for _, parts in columns)
    part_refs = refs[:taken]
    out_ref, grad_v, hidden_v, grad_sem, hidden_sems = refs[-5:]
    rows = grad_v.shape[1]
    load_grad = pltpu.make_async_copy(grad_ref.at[slot], grad_v, grad_sem)
    load_grad.start()
    loads = []
    at = 0
    for i, (_, parts) in enumerate(columns):
        for core, start, size in parts:
            load = pltpu.make_async_copy(
                part_refs[at],
                hidden_v.at[i, pl.ds(start, size), pl.ds(core * LANES, LANES)],
                hidden_sems.at[at],
            )
            load.start()
            loads.append((i, load))
            at += 1
    load_grad.wait()
    live = lax.broadcasted_iota(jnp.int32, (PIECE, rows), 1) < counts_ref[slot]
    for r in range(ROW_CUTS):
        cut = grad_v[pl.ds(r * PIECE, PIECE), :]
        grad_v[pl.ds(r * PIECE, PIECE), :] = jnp.where(live, cut, jnp.zeros_like(cut))
    x_here = place_ref[0] // 2
    core_here = lax.rem(place_ref[0], 2)
    for i, (step, _) in enumerate(columns):
        for j, load in loads:
            if i == j:
                load.wait()
        product = jnp.dot(grad_v[...], hidden_v[i], preferred_element_type=jnp.float32)
        product = product.astype(out_ref.dtype)
        x_there = lax.rem(x_here + step, COL_CUTS // 2)
        for c in range(2):
            column = 2 * x_there + (core_here if c == 0 else 1 - core_here)
            for r in range(ROW_CUTS):
                out_ref[r * COL_CUTS + column] = product[
                    r * PIECE : (r + 1) * PIECE, c * LANES : (c + 1) * LANES
                ]


def grad_far_kernel(slot, columns, place_ref, counts_ref, grad_ref, *refs):
    *inner, near_ref, out_ref, stage, grad_v, hidden_v, grad_sem, hidden_sems, out_sems = refs
    del near_ref
    grad_kernel(
        slot, columns, place_ref, counts_ref, grad_ref, *inner, stage, grad_v, hidden_v, grad_sem, hidden_sems
    )
    x_there = lax.rem(place_ref[0] // 2 + columns[0][0], COL_CUTS // 2)
    stores = []
    for r in range(ROW_CUTS):
        pair = pl.ds(r * COL_CUTS + 2 * x_there, 2)
        stores.append(pltpu.make_async_copy(stage.at[pair], out_ref.at[pair], out_sems.at[r]))
    for store in stores:
        store.start()
    for store in stores:
        store.wait()


def slot_gradient(slot, place, counts, grad_t, columns, near=None):
    rows = grad_t.shape[2]
    width = grad_t.shape[1]
    parts = [part for _, shard in columns for _, _, part in shard]
    plan = tuple(
        (step, tuple((core, start, part.shape[0]) for core, start, part in shard)) for step, shard in columns
    )
    piece_shape = (ROW_CUTS * COL_CUTS, PIECE, LANES)
    scratch = [
        pltpu.VMEM((width, rows), jnp.bfloat16),
        pltpu.VMEM((len(plan), rows, 2 * LANES), jnp.bfloat16),
        pltpu.SemaphoreType.DMA,
        pltpu.SemaphoreType.DMA((len(parts),)),
    ]
    specs = [smem_spec(), smem_spec()] + [any_spec()] * (1 + len(parts))
    cost = pl.CostEstimate(
        flops=2 * width * rows * 256 * len(plan), bytes_accessed=(2_000_000 + 38_000_000 * slot) * len(plan), transcendentals=0
    )
    if near is None:
        return pl.pallas_call(
            functools.partial(grad_kernel, slot, plan),
            out_shape=jax.ShapeDtypeStruct(piece_shape, jnp.bfloat16),
            in_specs=specs,
            out_specs=pl.BlockSpec(memory_space=pltpu.VMEM),
            scratch_shapes=scratch,
            compiler_params=pltpu.CompilerParams(vmem_limit_bytes=VMEM),
            cost_estimate=cost,
            name="gradient_near",
        )(place, counts, grad_t, *parts)
    return pl.pallas_call(
        functools.partial(grad_far_kernel, slot, plan),
        out_shape=jax.ShapeDtypeStruct(piece_shape, jnp.bfloat16),
        in_specs=specs + [any_spec()],
        out_specs=any_spec(),
        scratch_shapes=[pltpu.VMEM(piece_shape, jnp.bfloat16)]
        + scratch
        + [pltpu.SemaphoreType.DMA((ROW_CUTS,))],
        input_output_aliases={3 + len(parts): 0},
        compiler_params=pltpu.CompilerParams(vmem_limit_bytes=VMEM_FAR),
        cost_estimate=cost,
        name="gradient_far",
    )(place, counts, grad_t, *parts, near)


def list_length(lists_ref, e):
    length = jnp.int32(0)
    for j in range(lists_ref.shape[1]):
        length = length + (lists_ref[e, j] >= 0).astype(jnp.int32)
    return length


def sum_kernel(replicas_ref, owners_ref, first_ref, second_ref, out_ref, held, sems):
    loads = [
        pltpu.make_async_copy(src, held.at[s], sems.at[s])
        for s, src in enumerate((first_ref, second_ref))
    ]
    for load in loads:
        load.start()
    for load in loads:
        load.wait()

    @pl.loop(0, replicas_ref.shape[0])
    def _(e):
        def add(j, total):
            g = replicas_ref[e, j]
            return total + held[lax.rem(g, 2), g // 2].astype(jnp.float32)

        total = lax.fori_loop(
            0, list_length(replicas_ref, e), add, jnp.zeros((PIECE, LANES), jnp.float32)
        )
        out_ref[owners_ref[e]] = total.astype(out_ref.dtype)


def sum_copies(replicas, owner_map, first, second):
    pieces = first.shape[0]
    return pl.pallas_call(
        sum_kernel,
        out_shape=jax.ShapeDtypeStruct((pieces, PIECE, LANES), jnp.bfloat16),
        in_specs=[smem_spec(), smem_spec(), any_spec(), any_spec()],
        out_specs=pl.BlockSpec(memory_space=pltpu.VMEM),
        scratch_shapes=[
            pltpu.VMEM((2, pieces, PIECE, LANES), jnp.bfloat16),
            pltpu.SemaphoreType.DMA((2,)),
        ],
        compiler_params=pltpu.CompilerParams(vmem_limit_bytes=VMEM),
        name="sum_copies",
    )(replicas, owner_map, first, second)


def adam_cut(c, grad_ref, master_ref, first_ref, second_ref):
    cut = pl.ds(c * LANES, LANES)
    gradient = grad_ref[c].astype(jnp.float32)
    first_new = beta_first * first_ref[0, :, cut].astype(jnp.float32) + (1.0 - beta_first) * gradient
    second_new = (
        beta_second * second_ref[0, :, cut].astype(jnp.float32) + (1.0 - beta_second) * gradient * gradient
    )
    updated = master_ref[0, :, cut] - learn_rate * first_new / (jnp.sqrt(second_new) + adam_epsilon)
    return cut, first_new, second_new, updated


def weights_kernel(grad_ref, master_ref, first_ref, second_ref, sent_ref):
    for c in range(COL_CUTS):
        _, _, _, updated = adam_cut(c, grad_ref, master_ref, first_ref, second_ref)
        sent_ref[c] = updated.astype(sent_ref.dtype)


def state_kernel(grad_ref, master_ref, first_ref, second_ref, master_out, first_out, second_out):
    for c in range(COL_CUTS):
        cut, first_new, second_new, updated = adam_cut(c, grad_ref, master_ref, first_ref, second_ref)
        master_out[0, :, cut] = updated
        first_out[0, :, cut] = first_new.astype(first_out.dtype)
        second_out[0, :, cut] = second_new.astype(second_out.dtype)


def adam_update(kernel, name, kinds, gradient, master, first_moment, second_moment):
    rows = pl.BlockSpec((1, PIECE, COL_CUTS * LANES), lambda r: (0, r, 0))
    pieces = pl.BlockSpec((COL_CUTS, PIECE, LANES), lambda r: (r, 0, 0))
    if kinds is None:
        shapes = jax.ShapeDtypeStruct(gradient.shape, jnp.bfloat16)
        out_specs = pieces
    else:
        shapes = tuple(jax.ShapeDtypeStruct(master.shape, kind) for kind in kinds)
        out_specs = (rows,) * len(kinds)
    return pl.pallas_call(
        kernel,
        grid=(ROW_CUTS,),
        out_shape=shapes,
        in_specs=[pieces, rows, rows, rows],
        out_specs=out_specs,
        compiler_params=pltpu.CompilerParams(vmem_limit_bytes=VMEM),
        cost_estimate=pl.CostEstimate(flops=8_000_000, bytes_accessed=9_000_000, transcendentals=0),
        name=name,
    )(gradient, master, first_moment, second_moment)


def spread_kernel(lists_ref, owners_ref, weights_ref, out_ref, sem):
    @pl.loop(0, lists_ref.shape[0])
    def _(e):
        weights = weights_ref.at[owners_ref[e]]

        def put(j, carry):
            g = lists_ref[e, j]
            pltpu.make_async_copy(weights, out_ref.at[g // 2, lax.rem(g, 2)], sem).start()
            return carry

        lax.fori_loop(0, list_length(lists_ref, e), put, 0)

    pltpu.make_async_copy(out_ref, out_ref, sem).wait()


def spread_copies(next_replicas, owner_map, weights):
    pieces = weights.shape[0]
    return pl.pallas_call(
        spread_kernel,
        out_shape=jax.ShapeDtypeStruct((pieces, 2, PIECE, LANES), jnp.bfloat16),
        in_specs=[smem_spec(), smem_spec(), any_spec()],
        out_specs=any_spec(),
        scratch_shapes=[pltpu.SemaphoreType.DMA],
        compiler_params=pltpu.CompilerParams(vmem_limit_bytes=VMEM_ALL),
        name="spread_copies",
    )(next_replicas, owner_map, weights)


def order_kernel(pieces_ref, out_ref, sems):
    moves = []
    for s in range(2):
        for c in range(COL_CUTS):
            moves.append(
                pltpu.make_async_copy(
                    pieces_ref.at[:, c, s],
                    out_ref.at[s, :, :, pl.ds(c * LANES, LANES)],
                    sems.at[s, c],
                )
            )
    for move in moves:
        move.start()
    for move in moves:
        move.wait()


def order_pieces(pieces):
    width = ROW_CUTS * PIECE
    ordered = pl.pallas_call(
        order_kernel,
        out_shape=jax.ShapeDtypeStruct((2, ROW_CUTS, PIECE, COL_CUTS * LANES), jnp.bfloat16),
        in_specs=[any_spec()],
        out_specs=any_spec(),
        scratch_shapes=[pltpu.SemaphoreType.DMA((2, COL_CUTS))],
        compiler_params=pltpu.CompilerParams(vmem_limit_bytes=VMEM),
        name="order_pieces",
    )(pieces.reshape(ROW_CUTS, COL_CUTS, 2, PIECE, LANES))
    return ordered.reshape(2, width, COL_CUTS * LANES)


def x_shift(array, step):
    pairs = [(2 * x + c, 2 * ((x + step) % 4) + c) for x in range(4) for c in range(2)]
    return lax.ppermute(array, "dp", pairs)


def core_swap(array):
    pairs = [(2 * x + c, 2 * x + 1 - c) for x in range(4) for c in range(2)]
    return lax.ppermute(array, "dp", pairs)


def gather_near(own):
    half = own.shape[0] // 2
    ahead = x_shift(own, -1)
    behind = x_shift(own, 1)
    far = (x_shift(behind[:half], 1), x_shift(ahead[half:], -1))
    near = [
        (step, [(0, 0, shard), (1, 0, core_swap(shard))])
        for step, shard in ((0, own), (1, ahead), (3, behind))
    ]
    return near, far, (ahead, behind)


def gather_far(far):
    top, end = far
    half = top.shape[0]
    return [(2, [(0, 0, top), (1, 0, core_swap(top)), (0, half, end), (1, half, core_swap(end))])]


def exchange(pieces):
    return lax.all_to_all(pieces, "ep", split_axis=0, concat_axis=0, tiled=True)


def shards(
    hidden_rows,
    out_grad,
    row_counts,
    replicas,
    next_replicas,
    owner_map,
    master,
    first_moment,
    second_moment,
):
    place = lax.axis_index("dp").reshape(1).astype(jnp.int32)
    grad_t = jnp.swapaxes(out_grad, 1, 2)
    near, far, arrived = gather_near(hidden_rows[0])
    own_later, *_ = lax.optimization_barrier((hidden_rows[1], *arrived))
    near_later, far_later, hop_later = gather_near(own_later)
    pieces = slot_gradient(0, place, row_counts, grad_t, near)
    pieces, *far = lax.optimization_barrier((pieces, *far))
    pieces = slot_gradient(0, place, row_counts, grad_t, gather_far(far), pieces)
    pieces, *_ = lax.optimization_barrier((pieces, *hop_later))
    received_first = exchange(pieces)
    pieces = slot_gradient(1, place, row_counts, grad_t, near_later)
    pieces, *far = lax.optimization_barrier((pieces, *far_later))
    received_second = exchange(slot_gradient(1, place, row_counts, grad_t, gather_far(far), pieces))
    owner_pieces = sum_copies(replicas, owner_map, received_first, received_second)
    gradient = exchange(owner_pieces)
    state = (gradient, master, first_moment, second_moment)
    weight_pieces = adam_update(weights_kernel, "new_weights", None, *state)
    updated, new_first, new_second = adam_update(
        state_kernel, "new_state", (jnp.float32, jnp.bfloat16, jnp.bfloat16), *state
    )
    copies = spread_copies(next_replicas, owner_map, exchange(weight_pieces))
    next_copies = order_pieces(exchange(copies))
    return (updated, new_first, new_second, next_copies)


def solution(mesh):
    placed = (
        P("ep", None, "dp"),
        P("ep", None, "dp"),
        P("ep"),
        P(),
        P(),
        P(),
        P("ep", "dp", None),
        P("ep", "dp", None),
        P("ep", "dp", None),
    )
    return jax.shard_map(
        shards,
        mesh=mesh,
        in_specs=placed,
        out_specs=(
            P("ep", "dp", None),
            P("ep", "dp", None),
            P("ep", "dp", None),
            P("ep", "dp", None),
        ),
        check_vma=False,
    )
```

```python
import functools

import jax
import jax.numpy as jnp
from jax import lax
from jax.experimental import pallas as pl
from jax.experimental.pallas import tpu as pltpu
from jax.sharding import PartitionSpec as P

beta_first = 0.9
beta_second = 0.95
learn_rate = 0.001
adam_epsilon = 1e-08

ROW_CUTS = 4
COL_CUTS = 8
PIECE = 112
LANES = 128
VMEM = 48 * 1024 * 1024
VMEM_FAR = 48 * 1024 * 1024
VMEM_ALL = 62 * 1024 * 1024


def any_spec():
    return pl.BlockSpec(memory_space=pl.ANY)


def smem_spec():
    return pl.BlockSpec(memory_space=pltpu.SMEM)


def grad_kernel(slot, columns, place_ref, counts_ref, grad_ref, *refs):
    taken = sum(len(parts) for _, parts in columns)
    part_refs = refs[:taken]
    out_ref, grad_v, hidden_v, grad_sem, hidden_sems = refs[-5:]
    rows = grad_v.shape[1]
    load_grad = pltpu.make_async_copy(grad_ref.at[slot], grad_v, grad_sem)
    load_grad.start()
    loads = []
    at = 0
    for i, (_, parts) in enumerate(columns):
        for core, start, size in parts:
            load = pltpu.make_async_copy(
                part_refs[at],
                hidden_v.at[i, pl.ds(start, size), pl.ds(core * LANES, LANES)],
                hidden_sems.at[at],
            )
            load.start()
            loads.append((i, load))
            at += 1
    load_grad.wait()
    live = lax.broadcasted_iota(jnp.int32, (PIECE, rows), 1) < counts_ref[slot]
    for r in range(ROW_CUTS):
        cut = grad_v[pl.ds(r * PIECE, PIECE), :]
        grad_v[pl.ds(r * PIECE, PIECE), :] = jnp.where(live, cut, jnp.zeros_like(cut))
    x_here = place_ref[0] // 2
    core_here = lax.rem(place_ref[0], 2)
    for i, (step, _) in enumerate(columns):
        for j, load in loads:
            if i == j:
                load.wait()
        product = jnp.dot(grad_v[...], hidden_v[i], preferred_element_type=jnp.float32)
        product = product.astype(out_ref.dtype)
        x_there = lax.rem(x_here + step, COL_CUTS // 2)
        for c in range(2):
            column = 2 * x_there + (core_here if c == 0 else 1 - core_here)
            for r in range(ROW_CUTS):
                out_ref[r * COL_CUTS + column] = product[
                    r * PIECE : (r + 1) * PIECE, c * LANES : (c + 1) * LANES
                ]


def grad_far_kernel(slot, columns, place_ref, counts_ref, grad_ref, *refs):
    *inner, near_ref, out_ref, stage, grad_v, hidden_v, grad_sem, hidden_sems, out_sems = refs
    del near_ref
    grad_kernel(
        slot, columns, place_ref, counts_ref, grad_ref, *inner, stage, grad_v, hidden_v, grad_sem, hidden_sems
    )
    x_there = lax.rem(place_ref[0] // 2 + columns[0][0], COL_CUTS // 2)
    stores = []
    for r in range(ROW_CUTS):
        pair = pl.ds(r * COL_CUTS + 2 * x_there, 2)
        stores.append(pltpu.make_async_copy(stage.at[pair], out_ref.at[pair], out_sems.at[r]))
    for store in stores:
        store.start()
    for store in stores:
        store.wait()


def slot_gradient(slot, place, counts, grad_t, columns, near=None):
    rows = grad_t.shape[2]
    width = grad_t.shape[1]
    parts = [part for _, shard in columns for _, _, part in shard]
    plan = tuple(
        (step, tuple((core, start, part.shape[0]) for core, start, part in shard)) for step, shard in columns
    )
    piece_shape = (ROW_CUTS * COL_CUTS, PIECE, LANES)
    scratch = [
        pltpu.VMEM((width, rows), jnp.bfloat16),
        pltpu.VMEM((len(plan), rows, 2 * LANES), jnp.bfloat16),
        pltpu.SemaphoreType.DMA,
        pltpu.SemaphoreType.DMA((len(parts),)),
    ]
    specs = [smem_spec(), smem_spec()] + [any_spec()] * (1 + len(parts))
    cost = pl.CostEstimate(
        flops=2 * width * rows * 256 * len(plan), bytes_accessed=(2_000_000 + 38_000_000 * slot) * len(plan), transcendentals=0
    )
    if near is None:
        return pl.pallas_call(
            functools.partial(grad_kernel, slot, plan),
            out_shape=jax.ShapeDtypeStruct(piece_shape, jnp.bfloat16),
            in_specs=specs,
            out_specs=pl.BlockSpec(memory_space=pltpu.VMEM),
            scratch_shapes=scratch,
            compiler_params=pltpu.CompilerParams(vmem_limit_bytes=VMEM),
            cost_estimate=cost,
            name="gradient_near",
        )(place, counts, grad_t, *parts)
    return pl.pallas_call(
        functools.partial(grad_far_kernel, slot, plan),
        out_shape=jax.ShapeDtypeStruct(piece_shape, jnp.bfloat16),
        in_specs=specs + [any_spec()],
        out_specs=any_spec(),
        scratch_shapes=[pltpu.VMEM(piece_shape, jnp.bfloat16)]
        + scratch
        + [pltpu.SemaphoreType.DMA((ROW_CUTS,))],
        input_output_aliases={3 + len(parts): 0},
        compiler_params=pltpu.CompilerParams(vmem_limit_bytes=VMEM_FAR),
        cost_estimate=cost,
        name="gradient_far",
    )(place, counts, grad_t, *parts, near)


def list_length(lists_ref, e):
    length = jnp.int32(0)
    for j in range(lists_ref.shape[1]):
        length = length + (lists_ref[e, j] >= 0).astype(jnp.int32)
    return length


def sum_kernel(replicas_ref, owners_ref, first_ref, second_ref, out_ref, held, sems):
    loads = [
        pltpu.make_async_copy(src, held.at[s], sems.at[s])
        for s, src in enumerate((first_ref, second_ref))
    ]
    for load in loads:
        load.start()
    for load in loads:
        load.wait()

    @pl.loop(0, replicas_ref.shape[0])
    def _(e):
        def add(j, total):
            g = replicas_ref[e, j]
            return total + held[lax.rem(g, 2), g // 2].astype(jnp.float32)

        total = lax.fori_loop(
            0, list_length(replicas_ref, e), add, jnp.zeros((PIECE, LANES), jnp.float32)
        )
        out_ref[owners_ref[e]] = total.astype(out_ref.dtype)


def sum_copies(replicas, owner_map, first, second):
    pieces = first.shape[0]
    return pl.pallas_call(
        sum_kernel,
        out_shape=jax.ShapeDtypeStruct((pieces, PIECE, LANES), jnp.bfloat16),
        in_specs=[smem_spec(), smem_spec(), any_spec(), any_spec()],
        out_specs=pl.BlockSpec(memory_space=pltpu.VMEM),
        scratch_shapes=[
            pltpu.VMEM((2, pieces, PIECE, LANES), jnp.bfloat16),
            pltpu.SemaphoreType.DMA((2,)),
        ],
        compiler_params=pltpu.CompilerParams(vmem_limit_bytes=VMEM),
        name="sum_copies",
    )(replicas, owner_map, first, second)


def adam_cut(c, grad_ref, master_ref, first_ref, second_ref):
    cut = pl.ds(c * LANES, LANES)
    gradient = grad_ref[c].astype(jnp.float32)
    first_new = beta_first * first_ref[0, :, cut].astype(jnp.float32) + (1.0 - beta_first) * gradient
    second_new = (
        beta_second * second_ref[0, :, cut].astype(jnp.float32) + (1.0 - beta_second) * gradient * gradient
    )
    updated = master_ref[0, :, cut] - learn_rate * first_new / (jnp.sqrt(second_new) + adam_epsilon)
    return cut, first_new, second_new, updated


def weights_kernel(grad_ref, master_ref, first_ref, second_ref, sent_ref):
    for c in range(COL_CUTS):
        _, _, _, updated = adam_cut(c, grad_ref, master_ref, first_ref, second_ref)
        sent_ref[c] = updated.astype(sent_ref.dtype)


def state_kernel(grad_ref, master_ref, first_ref, second_ref, master_out, first_out, second_out):
    for c in range(COL_CUTS):
        cut, first_new, second_new, updated = adam_cut(c, grad_ref, master_ref, first_ref, second_ref)
        master_out[0, :, cut] = updated
        first_out[0, :, cut] = first_new.astype(first_out.dtype)
        second_out[0, :, cut] = second_new.astype(second_out.dtype)


def adam_update(kernel, name, kinds, gradient, master, first_moment, second_moment):
    rows = pl.BlockSpec((1, PIECE, COL_CUTS * LANES), lambda r: (0, r, 0))
    pieces = pl.BlockSpec((COL_CUTS, PIECE, LANES), lambda r: (r, 0, 0))
    if kinds is None:
        shapes = jax.ShapeDtypeStruct(gradient.shape, jnp.bfloat16)
        out_specs = pieces
    else:
        shapes = tuple(jax.ShapeDtypeStruct(master.shape, kind) for kind in kinds)
        out_specs = (rows,) * len(kinds)
    return pl.pallas_call(
        kernel,
        grid=(ROW_CUTS,),
        out_shape=shapes,
        in_specs=[pieces, rows, rows, rows],
        out_specs=out_specs,
        compiler_params=pltpu.CompilerParams(vmem_limit_bytes=VMEM),
        cost_estimate=pl.CostEstimate(flops=8_000_000, bytes_accessed=9_000_000, transcendentals=0),
        name=name,
    )(gradient, master, first_moment, second_moment)


def spread_kernel(lists_ref, owners_ref, weights_ref, out_ref):
    @pl.loop(0, lists_ref.shape[0])
    def _(e):
        weights = weights_ref[owners_ref[e]]

        def put(j, carry):
            g = lists_ref[e, j]
            out_ref[g // 2, lax.rem(g, 2)] = weights
            return carry

        lax.fori_loop(0, list_length(lists_ref, e), put, 0)


def spread_copies(next_replicas, owner_map, weights):
    pieces = weights.shape[0]
    return pl.pallas_call(
        spread_kernel,
        out_shape=jax.ShapeDtypeStruct((pieces, 2, PIECE, LANES), jnp.bfloat16),
        in_specs=[smem_spec(), smem_spec(), pl.BlockSpec(memory_space=pltpu.VMEM)],
        out_specs=pl.BlockSpec(memory_space=pltpu.VMEM),
        compiler_params=pltpu.CompilerParams(vmem_limit_bytes=VMEM_ALL),
        name="spread_copies",
    )(next_replicas, owner_map, weights)


def order_kernel(pieces_ref, out_ref):
    for s in range(2):
        for c in range(COL_CUTS):
            out_ref[s, :, pl.ds(c * LANES, LANES)] = pieces_ref[c, s]


def order_pieces(pieces):
    width = ROW_CUTS * PIECE
    return pl.pallas_call(
        order_kernel,
        grid=(ROW_CUTS,),
        out_shape=jax.ShapeDtypeStruct((2, width, COL_CUTS * LANES), jnp.bfloat16),
        in_specs=[pl.BlockSpec((COL_CUTS, 2, PIECE, LANES), lambda r: (r, 0, 0, 0))],
        out_specs=pl.BlockSpec((2, PIECE, COL_CUTS * LANES), lambda r: (0, r, 0)),
        compiler_params=pltpu.CompilerParams(vmem_limit_bytes=VMEM),
        name="order_pieces",
    )(pieces)


def x_shift(array, step):
    pairs = [(2 * x + c, 2 * ((x + step) % 4) + c) for x in range(4) for c in range(2)]
    return lax.ppermute(array, "dp", pairs)


def core_swap(array):
    pairs = [(2 * x + c, 2 * x + 1 - c) for x in range(4) for c in range(2)]
    return lax.ppermute(array, "dp", pairs)


def gather_near(own):
    half = own.shape[0] // 2
    ahead = x_shift(own, -1)
    behind = x_shift(own, 1)
    far = (x_shift(behind[:half], 1), x_shift(ahead[half:], -1))
    near = [
        (step, [(0, 0, shard), (1, 0, core_swap(shard))])
        for step, shard in ((0, own), (1, ahead), (3, behind))
    ]
    return near, far, (ahead, behind)


def gather_far(far):
    top, end = far
    half = top.shape[0]
    return [(2, [(0, 0, top), (1, 0, core_swap(top)), (0, half, end), (1, half, core_swap(end))])]


def exchange(pieces):
    return lax.all_to_all(pieces, "ep", split_axis=0, concat_axis=0, tiled=True)


def shards(
    hidden_rows,
    out_grad,
    row_counts,
    replicas,
    next_replicas,
    owner_map,
    master,
    first_moment,
    second_moment,
):
    place = lax.axis_index("dp").reshape(1).astype(jnp.int32)
    grad_t = jnp.swapaxes(out_grad, 1, 2)
    near, far, arrived = gather_near(hidden_rows[0])
    own_later, *_ = lax.optimization_barrier((hidden_rows[1], *arrived))
    near_later, far_later, hop_later = gather_near(own_later)
    pieces = slot_gradient(0, place, row_counts, grad_t, near)
    pieces, *far = lax.optimization_barrier((pieces, *far))
    pieces = slot_gradient(0, place, row_counts, grad_t, gather_far(far), pieces)
    pieces, *_ = lax.optimization_barrier((pieces, *hop_later))
    received_first = exchange(pieces)
    pieces = slot_gradient(1, place, row_counts, grad_t, near_later)
    pieces, *far = lax.optimization_barrier((pieces, *far_later))
    received_second = exchange(slot_gradient(1, place, row_counts, grad_t, gather_far(far), pieces))
    owner_pieces = sum_copies(replicas, owner_map, received_first, received_second)
    gradient = exchange(owner_pieces)
    state = (gradient, master, first_moment, second_moment)
    weight_pieces = adam_update(weights_kernel, "new_weights", None, *state)
    updated, new_first, new_second = adam_update(
        state_kernel, "new_state", (jnp.float32, jnp.bfloat16, jnp.bfloat16), *state
    )
    copies = spread_copies(next_replicas, owner_map, exchange(weight_pieces))
    next_copies = order_pieces(exchange(copies))
    return (updated, new_first, new_second, next_copies)


def solution(mesh):
    placed = (
        P("ep", None, "dp"),
        P("ep", None, "dp"),
        P("ep"),
        P(),
        P(),
        P(),
        P("ep", "dp", None),
        P("ep", "dp", None),
        P("ep", "dp", None),
    )
    return jax.shard_map(
        shards,
        mesh=mesh,
        in_specs=placed,
        out_specs=(
            P("ep", "dp", None),
            P("ep", "dp", None),
            P("ep", "dp", None),
            P("ep", "dp", None),
        ),
        check_vma=False,
    )
```

```python
import functools

import jax
import jax.numpy as jnp
from jax import lax
from jax.experimental import pallas as pl
from jax.experimental.pallas import tpu as pltpu
from jax.sharding import PartitionSpec as P

beta_first = 0.9
beta_second = 0.95
learn_rate = 0.001
adam_epsilon = 1e-08

ROW_CUTS = 4
COL_CUTS = 8
LEAD = 1
PIECE = 112
LANES = 128
VMEM = 48 * 1024 * 1024
VMEM_FAR = 48 * 1024 * 1024
VMEM_LOW = 16 * 1024 * 1024
VMEM_ALL = 62 * 1024 * 1024


def any_spec():
    return pl.BlockSpec(memory_space=pl.ANY)


def smem_spec():
    return pl.BlockSpec(memory_space=pltpu.SMEM)


def grad_kernel(slot, columns, place_ref, counts_ref, grad_ref, *refs):
    taken = sum(choices for _, parts in columns for *_, choices in parts)
    part_refs = refs[:taken]
    out_ref, grad_v, hidden_v, grad_sem, hidden_sems = refs[-5:]
    rows = grad_v.shape[1]
    load_grad = pltpu.make_async_copy(grad_ref.at[slot], grad_v, grad_sem)
    load_grad.start()
    core_here = lax.rem(place_ref[0], 2)
    loads = []
    at = 0
    for i, (_, parts) in enumerate(columns):
        for core, start, size, choices in parts:
            into = hidden_v.at[i, pl.ds(start, size), pl.ds(core * LANES, LANES)]
            choice = [
                pltpu.make_async_copy(part_refs[at + k], into, hidden_sems.at[at]) for k in range(choices)
            ]
            if choices == 1:
                choice[0].start()
            else:
                pl.when(core_here == LEAD)(choice[0].start)
                pl.when(core_here != LEAD)(choice[1].start)
            loads.append((i, choice[0]))
            at += choices
    load_grad.wait()
    live = lax.broadcasted_iota(jnp.int32, (PIECE, rows), 1) < counts_ref[slot]
    for r in range(ROW_CUTS):
        cut = grad_v[pl.ds(r * PIECE, PIECE), :]
        grad_v[pl.ds(r * PIECE, PIECE), :] = jnp.where(live, cut, jnp.zeros_like(cut))
    x_here = place_ref[0] // 2
    for i, (step, _) in enumerate(columns):
        for j, load in loads:
            if i == j:
                load.wait()
        product = jnp.dot(grad_v[...], hidden_v[i], preferred_element_type=jnp.float32)
        product = product.astype(out_ref.dtype)
        x_there = lax.rem(x_here + step, COL_CUTS // 2)
        for c in range(2):
            column = 2 * x_there + (core_here if c == 0 else 1 - core_here)
            for r in range(ROW_CUTS):
                out_ref[r * COL_CUTS + column] = product[
                    r * PIECE : (r + 1) * PIECE, c * LANES : (c + 1) * LANES
                ]


def grad_far_kernel(slot, columns, place_ref, counts_ref, grad_ref, *refs):
    *inner, near_ref, out_ref, stage, grad_v, hidden_v, grad_sem, hidden_sems, out_sems = refs
    del near_ref
    grad_kernel(
        slot, columns, place_ref, counts_ref, grad_ref, *inner, stage, grad_v, hidden_v, grad_sem, hidden_sems
    )
    x_there = lax.rem(place_ref[0] // 2 + columns[0][0], COL_CUTS // 2)
    stores = []
    for r in range(ROW_CUTS):
        pair = pl.ds(r * COL_CUTS + 2 * x_there, 2)
        stores.append(pltpu.make_async_copy(stage.at[pair], out_ref.at[pair], out_sems.at[r]))
    for store in stores:
        store.start()
    for store in stores:
        store.wait()


def slot_gradient(slot, place, counts, grad_t, columns, near=None):
    rows = grad_t.shape[2]
    width = grad_t.shape[1]
    parts = [part for _, shard in columns for _, _, *choices in shard for part in choices]
    plan = tuple(
        (step, tuple((core, start, part[0].shape[0], len(part)) for core, start, *part in shard))
        for step, shard in columns
    )
    piece_shape = (ROW_CUTS * COL_CUTS, PIECE, LANES)
    scratch = [
        pltpu.VMEM((width, rows), jnp.bfloat16),
        pltpu.VMEM((len(plan), rows, 2 * LANES), jnp.bfloat16),
        pltpu.SemaphoreType.DMA,
        pltpu.SemaphoreType.DMA((len(parts),)),
    ]
    specs = [smem_spec(), smem_spec()] + [any_spec()] * (1 + len(parts))
    cost = pl.CostEstimate(
        flops=2 * width * rows * 256 * len(plan), bytes_accessed=(2_000_000 + 38_000_000 * slot) * len(plan), transcendentals=0
    )
    if near is None:
        return pl.pallas_call(
            functools.partial(grad_kernel, slot, plan),
            out_shape=jax.ShapeDtypeStruct(piece_shape, jnp.bfloat16),
            in_specs=specs,
            out_specs=pl.BlockSpec(memory_space=pltpu.VMEM),
            scratch_shapes=scratch,
            compiler_params=pltpu.CompilerParams(vmem_limit_bytes=VMEM),
            cost_estimate=cost,
            name="gradient_near",
        )(place, counts, grad_t, *parts)
    return pl.pallas_call(
        functools.partial(grad_far_kernel, slot, plan),
        out_shape=jax.ShapeDtypeStruct(piece_shape, jnp.bfloat16),
        in_specs=specs + [any_spec()],
        out_specs=any_spec(),
        scratch_shapes=[pltpu.VMEM(piece_shape, jnp.bfloat16)]
        + scratch
        + [pltpu.SemaphoreType.DMA((ROW_CUTS,))],
        input_output_aliases={3 + len(parts): 0},
        compiler_params=pltpu.CompilerParams(vmem_limit_bytes=VMEM_FAR),
        cost_estimate=cost,
        name="gradient_far",
    )(place, counts, grad_t, *parts, near)


def list_length(lists_ref, e):
    length = jnp.int32(0)
    for j in range(lists_ref.shape[1]):
        length = length + (lists_ref[e, j] >= 0).astype(jnp.int32)
    return length


def sum_kernel(replicas_ref, owners_ref, first_ref, second_ref, out_ref, held, sems):
    loads = [
        pltpu.make_async_copy(src, held.at[s], sems.at[s])
        for s, src in enumerate((first_ref, second_ref))
    ]
    for load in loads:
        load.start()
    for load in loads:
        load.wait()

    @pl.loop(0, replicas_ref.shape[0])
    def _(e):
        def add(j, total):
            g = replicas_ref[e, j]
            return total + held[lax.rem(g, 2), g // 2].astype(jnp.float32)

        total = lax.fori_loop(
            0, list_length(replicas_ref, e), add, jnp.zeros((PIECE, LANES), jnp.float32)
        )
        out_ref[owners_ref[e]] = total.astype(out_ref.dtype)


def sum_copies(replicas, owner_map, first, second):
    pieces = first.shape[0]
    return pl.pallas_call(
        sum_kernel,
        out_shape=jax.ShapeDtypeStruct((pieces, PIECE, LANES), jnp.bfloat16),
        in_specs=[smem_spec(), smem_spec(), any_spec(), any_spec()],
        out_specs=pl.BlockSpec(memory_space=pltpu.VMEM),
        scratch_shapes=[
            pltpu.VMEM((2, pieces, PIECE, LANES), jnp.bfloat16),
            pltpu.SemaphoreType.DMA((2,)),
        ],
        compiler_params=pltpu.CompilerParams(vmem_limit_bytes=VMEM),
        name="sum_copies",
    )(replicas, owner_map, first, second)


def adam_cut(c, grad_ref, master_ref, first_ref, second_ref):
    cut = pl.ds(c * LANES, LANES)
    gradient = grad_ref[c].astype(jnp.float32)
    first_new = beta_first * first_ref[0, :, cut].astype(jnp.float32) + (1.0 - beta_first) * gradient
    second_new = (
        beta_second * second_ref[0, :, cut].astype(jnp.float32) + (1.0 - beta_second) * gradient * gradient
    )
    updated = master_ref[0, :, cut] - learn_rate * first_new / (jnp.sqrt(second_new) + adam_epsilon)
    return cut, first_new, second_new, updated


def weights_kernel(grad_ref, master_ref, first_ref, second_ref, sent_ref):
    for c in range(COL_CUTS):
        _, _, _, updated = adam_cut(c, grad_ref, master_ref, first_ref, second_ref)
        sent_ref[c] = updated.astype(sent_ref.dtype)


def state_kernel(grad_ref, master_ref, first_ref, second_ref, master_out, first_out, second_out):
    for c in range(COL_CUTS):
        cut, first_new, second_new, updated = adam_cut(c, grad_ref, master_ref, first_ref, second_ref)
        master_out[0, :, cut] = updated
        first_out[0, :, cut] = first_new.astype(first_out.dtype)
        second_out[0, :, cut] = second_new.astype(second_out.dtype)


def adam_update(kernel, name, kinds, gradient, master, first_moment, second_moment):
    rows = pl.BlockSpec((1, PIECE, COL_CUTS * LANES), lambda r: (0, r, 0))
    pieces = pl.BlockSpec((COL_CUTS, PIECE, LANES), lambda r: (r, 0, 0))
    if kinds is None:
        shapes = jax.ShapeDtypeStruct(gradient.shape, jnp.bfloat16)
        out_specs = pieces
    else:
        shapes = tuple(jax.ShapeDtypeStruct(master.shape, kind) for kind in kinds)
        out_specs = (rows,) * len(kinds)
    return pl.pallas_call(
        kernel,
        grid=(ROW_CUTS,),
        out_shape=shapes,
        in_specs=[pieces, rows, rows, rows],
        out_specs=out_specs,
        compiler_params=pltpu.CompilerParams(vmem_limit_bytes=VMEM if kinds is None else VMEM_LOW),
        cost_estimate=pl.CostEstimate(flops=8_000_000, bytes_accessed=9_000_000, transcendentals=0),
        name=name,
    )(gradient, master, first_moment, second_moment)


def spread_kernel(lists_ref, owners_ref, weights_ref, out_ref, sem):
    @pl.loop(0, lists_ref.shape[0])
    def _(e):
        weights = weights_ref.at[owners_ref[e]]

        def put(j, carry):
            g = lists_ref[e, j]
            pltpu.make_async_copy(weights, out_ref.at[g // 2, lax.rem(g, 2)], sem).start()
            return carry

        lax.fori_loop(0, list_length(lists_ref, e), put, 0)

    pltpu.make_async_copy(out_ref, out_ref, sem).wait()


def spread_copies(next_replicas, owner_map, weights):
    pieces = weights.shape[0]
    return pl.pallas_call(
        spread_kernel,
        out_shape=jax.ShapeDtypeStruct((pieces, 2, PIECE, LANES), jnp.bfloat16),
        in_specs=[smem_spec(), smem_spec(), pl.BlockSpec(memory_space=pltpu.VMEM)],
        out_specs=any_spec(),
        scratch_shapes=[pltpu.SemaphoreType.DMA],
        compiler_params=pltpu.CompilerParams(vmem_limit_bytes=VMEM_ALL),
        name="spread_copies",
    )(next_replicas, owner_map, weights)


def order_kernel(pieces_ref, out_ref):
    for s in range(2):
        for c in range(COL_CUTS):
            out_ref[s, :, pl.ds(c * LANES, LANES)] = pieces_ref[c, s]


def order_pieces(pieces):
    width = ROW_CUTS * PIECE
    return pl.pallas_call(
        order_kernel,
        grid=(ROW_CUTS,),
        out_shape=jax.ShapeDtypeStruct((2, width, COL_CUTS * LANES), jnp.bfloat16),
        in_specs=[pl.BlockSpec((COL_CUTS, 2, PIECE, LANES), lambda r: (r, 0, 0, 0))],
        out_specs=pl.BlockSpec((2, PIECE, COL_CUTS * LANES), lambda r: (0, r, 0)),
        compiler_params=pltpu.CompilerParams(vmem_limit_bytes=VMEM_LOW),
        name="order_pieces",
    )(pieces)


def x_shift(array, step, cores=(0, 1)):
    pairs = [(2 * x + c, 2 * ((x + step) % 4) + c) for x in range(4) for c in cores]
    return lax.ppermute(array, "dp", pairs)


def core_swap(array):
    pairs = [(2 * x + c, 2 * x + 1 - c) for x in range(4) for c in range(2)]
    return lax.ppermute(array, "dp", pairs)


def gather_near(own, way):
    ahead = x_shift(own, -1)
    behind = x_shift(own, 1)
    far = x_shift(behind if way > 0 else ahead, way)
    near = [
        (step, [(0, 0, shard), (1, 0, core_swap(shard))])
        for step, shard in ((0, own), (1, ahead), (3, behind))
    ]
    return near, far, (ahead, behind)


def gather_far(far):
    return [(2, [(0, 0, far), (1, 0, core_swap(far))])]


def gather_far_apart(far, behind_swapped):
    to_lead = lax.ppermute(far, "dp", [(2 * x + 1 - LEAD, 2 * x + LEAD) for x in range(4)])
    return [(2, [(0, 0, far), (1, 0, to_lead, x_shift(behind_swapped, 1, (1 - LEAD,)))])]


def exchange(pieces):
    return lax.all_to_all(pieces, "ep", split_axis=0, concat_axis=0, tiled=True)


def shards(
    hidden_rows,
    out_grad,
    row_counts,
    replicas,
    next_replicas,
    owner_map,
    master,
    first_moment,
    second_moment,
):
    place = lax.axis_index("dp").reshape(1).astype(jnp.int32)
    grad_t = jnp.swapaxes(out_grad, 1, 2)
    near, far, arrived = gather_near(hidden_rows[0], 1)
    own_later, *_ = lax.optimization_barrier((hidden_rows[1], *arrived))
    near_later, far_later, _ = gather_near(own_later, -1)
    pieces = slot_gradient(0, place, row_counts, grad_t, near)
    pieces, far = lax.optimization_barrier((pieces, far))
    pieces = slot_gradient(0, place, row_counts, grad_t, gather_far(far), pieces)
    pieces, _ = lax.optimization_barrier((pieces, near_later[1][1][1][2]))
    received_first = exchange(pieces)
    columns = near_later + gather_far_apart(far_later, near_later[2][1][1][2])
    received_second = exchange(slot_gradient(1, place, row_counts, grad_t, columns))
    owner_pieces = sum_copies(replicas, owner_map, received_first, received_second)
    gradient = exchange(owner_pieces)
    state = (gradient, master, first_moment, second_moment)
    weight_pieces = adam_update(weights_kernel, "new_weights", None, *state)
    updated, new_first, new_second = adam_update(
        state_kernel, "new_state", (jnp.float32, jnp.bfloat16, jnp.bfloat16), *state
    )
    copies = spread_copies(next_replicas, owner_map, exchange(weight_pieces))
    next_copies = order_pieces(exchange(copies))
    return (updated, new_first, new_second, next_copies)


def solution(mesh):
    placed = (
        P("ep", None, "dp"),
        P("ep", None, "dp"),
        P("ep"),
        P(),
        P(),
        P(),
        P("ep", "dp", None),
        P("ep", "dp", None),
        P("ep", "dp", None),
    )
    return jax.shard_map(
        shards,
        mesh=mesh,
        in_specs=placed,
        out_specs=(
            P("ep", "dp", None),
            P("ep", "dp", None),
            P("ep", "dp", None),
            P("ep", "dp", None),
        ),
        check_vma=False,
    )
```

```python
import functools

import jax
import jax.numpy as jnp
from jax import lax
from jax.experimental import pallas as pl
from jax.experimental.pallas import tpu as pltpu
from jax.sharding import PartitionSpec as P

beta_first = 0.9
beta_second = 0.95
learn_rate = 0.001
adam_epsilon = 1e-08

ROW_CUTS = 4
COL_CUTS = 8
LEAD = 1
PIECE = 112
LANES = 128
VMEM = 48 * 1024 * 1024
VMEM_FAR = 48 * 1024 * 1024
VMEM_LOW = 16 * 1024 * 1024
VMEM_ALL = 62 * 1024 * 1024


def any_spec():
    return pl.BlockSpec(memory_space=pl.ANY)


def smem_spec():
    return pl.BlockSpec(memory_space=pltpu.SMEM)


def grad_kernel(slot, columns, place_ref, counts_ref, grad_ref, *refs):
    taken = sum(choices for _, parts in columns for *_, choices in parts)
    part_refs = refs[:taken]
    out_ref, grad_v, hidden_v, grad_sem, hidden_sems = refs[-5:]
    rows = grad_v.shape[1]
    load_grad = pltpu.make_async_copy(grad_ref.at[slot], grad_v, grad_sem)
    load_grad.start()
    core_here = lax.rem(place_ref[0], 2)
    loads = []
    at = 0
    for i, (_, parts) in enumerate(columns):
        for core, start, size, choices in parts:
            into = hidden_v.at[i, pl.ds(start, size), pl.ds(core * LANES, LANES)]
            choice = [
                pltpu.make_async_copy(part_refs[at + k], into, hidden_sems.at[at]) for k in range(choices)
            ]
            if choices == 1:
                choice[0].start()
            else:
                pl.when(core_here == LEAD)(choice[0].start)
                pl.when(core_here != LEAD)(choice[1].start)
            loads.append((i, choice[0]))
            at += choices
    load_grad.wait()
    live = lax.broadcasted_iota(jnp.int32, (PIECE, rows), 1) < counts_ref[slot]
    for r in range(ROW_CUTS):
        cut = grad_v[pl.ds(r * PIECE, PIECE), :]
        grad_v[pl.ds(r * PIECE, PIECE), :] = jnp.where(live, cut, jnp.zeros_like(cut))
    x_here = place_ref[0] // 2
    for _, load in loads:
        load.wait()

    @pl.loop(0, len(columns))
    def _(i):
        step = sum(jnp.where(i == k, there, 0) for k, (there, _) in enumerate(columns))
        product = jnp.dot(grad_v[...], hidden_v[i], preferred_element_type=jnp.float32)
        product = product.astype(out_ref.dtype)
        x_there = lax.rem(x_here + step, COL_CUTS // 2)
        for c in range(2):
            column = 2 * x_there + (core_here if c == 0 else 1 - core_here)
            for r in range(ROW_CUTS):
                out_ref[r * COL_CUTS + column] = product[
                    r * PIECE : (r + 1) * PIECE, c * LANES : (c + 1) * LANES
                ]


def grad_far_kernel(slot, columns, place_ref, counts_ref, grad_ref, *refs):
    *inner, near_ref, out_ref, stage, grad_v, hidden_v, grad_sem, hidden_sems, out_sems = refs
    del near_ref
    grad_kernel(
        slot, columns, place_ref, counts_ref, grad_ref, *inner, stage, grad_v, hidden_v, grad_sem, hidden_sems
    )
    x_there = lax.rem(place_ref[0] // 2 + columns[0][0], COL_CUTS // 2)
    stores = []
    for r in range(ROW_CUTS):
        pair = pl.ds(r * COL_CUTS + 2 * x_there, 2)
        stores.append(pltpu.make_async_copy(stage.at[pair], out_ref.at[pair], out_sems.at[r]))
    for store in stores:
        store.start()
    for store in stores:
        store.wait()


def slot_gradient(slot, place, counts, grad_t, columns, near=None):
    rows = grad_t.shape[2]
    width = grad_t.shape[1]
    parts = [part for _, shard in columns for _, _, *choices in shard for part in choices]
    plan = tuple(
        (step, tuple((core, start, part[0].shape[0], len(part)) for core, start, *part in shard))
        for step, shard in columns
    )
    piece_shape = (ROW_CUTS * COL_CUTS, PIECE, LANES)
    scratch = [
        pltpu.VMEM((width, rows), jnp.bfloat16),
        pltpu.VMEM((len(plan), rows, 2 * LANES), jnp.bfloat16),
        pltpu.SemaphoreType.DMA,
        pltpu.SemaphoreType.DMA((len(parts),)),
    ]
    specs = [smem_spec(), smem_spec()] + [any_spec()] * (1 + len(parts))
    cost = pl.CostEstimate(
        flops=2 * width * rows * 256 * len(plan), bytes_accessed=(2_000_000 + 38_000_000 * slot) * len(plan), transcendentals=0
    )
    if near is None:
        return pl.pallas_call(
            functools.partial(grad_kernel, slot, plan),
            out_shape=jax.ShapeDtypeStruct(piece_shape, jnp.bfloat16),
            in_specs=specs,
            out_specs=pl.BlockSpec(memory_space=pltpu.VMEM),
            scratch_shapes=scratch,
            compiler_params=pltpu.CompilerParams(vmem_limit_bytes=VMEM),
            cost_estimate=cost,
            name="gradient_near",
        )(place, counts, grad_t, *parts)
    return pl.pallas_call(
        functools.partial(grad_far_kernel, slot, plan),
        out_shape=jax.ShapeDtypeStruct(piece_shape, jnp.bfloat16),
        in_specs=specs + [any_spec()],
        out_specs=any_spec(),
        scratch_shapes=[pltpu.VMEM(piece_shape, jnp.bfloat16)]
        + scratch
        + [pltpu.SemaphoreType.DMA((ROW_CUTS,))],
        input_output_aliases={3 + len(parts): 0},
        compiler_params=pltpu.CompilerParams(vmem_limit_bytes=VMEM_FAR),
        cost_estimate=cost,
        name="gradient_far",
    )(place, counts, grad_t, *parts, near)


def list_length(lists_ref, e):
    length = jnp.int32(0)
    for j in range(lists_ref.shape[1]):
        length = length + (lists_ref[e, j] >= 0).astype(jnp.int32)
    return length


def sum_kernel(replicas_ref, owners_ref, first_ref, second_ref, out_ref, held, sems):
    loads = [
        pltpu.make_async_copy(src, held.at[s], sems.at[s])
        for s, src in enumerate((first_ref, second_ref))
    ]
    for load in loads:
        load.start()
    for load in loads:
        load.wait()

    @pl.loop(0, replicas_ref.shape[0])
    def _(e):
        def take(j):
            g = replicas_ref[e, j]
            return held[lax.rem(g, 2), g // 2].astype(jnp.float32)

        total = lax.fori_loop(
            1, list_length(replicas_ref, e), lambda j, total: total + take(j), take(0)
        )
        out_ref[owners_ref[e]] = total.astype(out_ref.dtype)


def sum_copies(replicas, owner_map, first, second):
    pieces = first.shape[0]
    return pl.pallas_call(
        sum_kernel,
        out_shape=jax.ShapeDtypeStruct((pieces, PIECE, LANES), jnp.bfloat16),
        in_specs=[smem_spec(), smem_spec(), any_spec(), any_spec()],
        out_specs=pl.BlockSpec(memory_space=pltpu.VMEM),
        scratch_shapes=[
            pltpu.VMEM((2, pieces, PIECE, LANES), jnp.bfloat16),
            pltpu.SemaphoreType.DMA((2,)),
        ],
        compiler_params=pltpu.CompilerParams(vmem_limit_bytes=VMEM),
        name="sum_copies",
    )(replicas, owner_map, first, second)


def adam_cut(c, grad_ref, master_ref, first_ref, second_ref):
    cut = pl.ds(c * LANES, LANES)
    gradient = grad_ref[c].astype(jnp.float32)
    first_new = beta_first * first_ref[0, :, cut].astype(jnp.float32) + (1.0 - beta_first) * gradient
    second_new = (
        beta_second * second_ref[0, :, cut].astype(jnp.float32) + (1.0 - beta_second) * gradient * gradient
    )
    updated = master_ref[0, :, cut] - learn_rate * first_new / (jnp.sqrt(second_new) + adam_epsilon)
    return cut, first_new, second_new, updated


def weights_kernel(grad_ref, master_ref, first_ref, second_ref, sent_ref):
    for c in range(COL_CUTS):
        _, _, _, updated = adam_cut(c, grad_ref, master_ref, first_ref, second_ref)
        sent_ref[c] = updated.astype(sent_ref.dtype)


def state_kernel(grad_ref, master_ref, first_ref, second_ref, master_out, first_out, second_out):
    for c in range(COL_CUTS):
        cut, first_new, second_new, updated = adam_cut(c, grad_ref, master_ref, first_ref, second_ref)
        master_out[0, :, cut] = updated
        first_out[0, :, cut] = first_new.astype(first_out.dtype)
        second_out[0, :, cut] = second_new.astype(second_out.dtype)


def adam_update(kernel, name, kinds, gradient, master, first_moment, second_moment):
    rows = pl.BlockSpec((1, PIECE, COL_CUTS * LANES), lambda r: (0, r, 0))
    pieces = pl.BlockSpec((COL_CUTS, PIECE, LANES), lambda r: (r, 0, 0))
    if kinds is None:
        shapes = jax.ShapeDtypeStruct(gradient.shape, jnp.bfloat16)
        out_specs = pieces
    else:
        shapes = tuple(jax.ShapeDtypeStruct(master.shape, kind) for kind in kinds)
        out_specs = (rows,) * len(kinds)
    return pl.pallas_call(
        kernel,
        grid=(ROW_CUTS,),
        out_shape=shapes,
        in_specs=[pieces, rows, rows, rows],
        out_specs=out_specs,
        compiler_params=pltpu.CompilerParams(vmem_limit_bytes=VMEM if kinds is None else VMEM_LOW),
        cost_estimate=pl.CostEstimate(flops=8_000_000, bytes_accessed=9_000_000, transcendentals=0),
        name=name,
    )(gradient, master, first_moment, second_moment)


def spread_kernel(lists_ref, owners_ref, weights_ref, out_ref, sem):
    @pl.loop(0, lists_ref.shape[0])
    def _(e):
        weights = weights_ref.at[owners_ref[e]]

        def put(j, carry):
            g = lists_ref[e, j]
            pltpu.make_async_copy(weights, out_ref.at[g // 2, lax.rem(g, 2)], sem).start()
            return carry

        lax.fori_loop(0, list_length(lists_ref, e), put, 0)

    pltpu.make_async_copy(out_ref, out_ref, sem).wait()


def spread_copies(next_replicas, owner_map, weights):
    pieces = weights.shape[0]
    return pl.pallas_call(
        spread_kernel,
        out_shape=jax.ShapeDtypeStruct((pieces, 2, PIECE, LANES), jnp.bfloat16),
        in_specs=[smem_spec(), smem_spec(), pl.BlockSpec(memory_space=pltpu.VMEM)],
        out_specs=any_spec(),
        scratch_shapes=[pltpu.SemaphoreType.DMA],
        compiler_params=pltpu.CompilerParams(vmem_limit_bytes=VMEM_ALL),
        name="spread_copies",
    )(next_replicas, owner_map, weights)


def order_kernel(pieces_ref, out_ref, ordered, load_sems, store_sems):
    loads = [
        [
            pltpu.make_async_copy(
                pieces_ref.at[r, c], ordered.at[:, r, :, pl.ds(c * LANES, LANES)], load_sems.at[r, c]
            )
            for c in range(COL_CUTS)
        ]
        for r in range(ROW_CUTS)
    ]
    for row in loads:
        for load in row:
            load.start()
    stores = []
    for r, row in enumerate(loads):
        for load in row:
            load.wait()
        store = pltpu.make_async_copy(ordered.at[:, r], out_ref.at[:, r], store_sems.at[r])
        store.start()
        stores.append(store)
    for store in stores:
        store.wait()


def order_pieces(pieces):
    shape = (2, ROW_CUTS, PIECE, COL_CUTS * LANES)
    return pl.pallas_call(
        order_kernel,
        out_shape=jax.ShapeDtypeStruct(shape, jnp.bfloat16),
        in_specs=[any_spec()],
        out_specs=any_spec(),
        scratch_shapes=[
            pltpu.VMEM(shape, jnp.bfloat16),
            pltpu.SemaphoreType.DMA((ROW_CUTS, COL_CUTS)),
            pltpu.SemaphoreType.DMA((ROW_CUTS,)),
        ],
        compiler_params=pltpu.CompilerParams(vmem_limit_bytes=VMEM_LOW),
        name="order_pieces",
    )(pieces.reshape(ROW_CUTS, COL_CUTS, 2, PIECE, LANES)).reshape(2, ROW_CUTS * PIECE, COL_CUTS * LANES)


def x_shift(array, step, cores=(0, 1)):
    pairs = [(2 * x + c, 2 * ((x + step) % 4) + c) for x in range(4) for c in cores]
    return lax.ppermute(array, "dp", pairs)


def core_swap(array):
    pairs = [(2 * x + c, 2 * x + 1 - c) for x in range(4) for c in range(2)]
    return lax.ppermute(array, "dp", pairs)


def gather_near(own, way):
    ahead = x_shift(own, -1)
    behind = x_shift(own, 1)
    far = x_shift(behind if way > 0 else ahead, way)
    near = [
        (step, [(0, 0, shard), (1, 0, core_swap(shard))])
        for step, shard in ((0, own), (1, ahead), (3, behind))
    ]
    return near, far, (ahead, behind)


def gather_far(far):
    return [(2, [(0, 0, far), (1, 0, core_swap(far))])]


def gather_far_apart(far, behind_swapped):
    to_lead = lax.ppermute(far, "dp", [(2 * x + 1 - LEAD, 2 * x + LEAD) for x in range(4)])
    return [(2, [(0, 0, far), (1, 0, to_lead, x_shift(behind_swapped, 1, (1 - LEAD,)))])]


def exchange(pieces):
    return lax.all_to_all(pieces, "ep", split_axis=0, concat_axis=0, tiled=True)


def shards(
    hidden_rows,
    out_grad,
    row_counts,
    replicas,
    next_replicas,
    owner_map,
    master,
    first_moment,
    second_moment,
):
    place = lax.axis_index("dp").reshape(1).astype(jnp.int32)
    grad_t = jnp.swapaxes(out_grad, 1, 2)
    near, far, arrived = gather_near(hidden_rows[0], 1)
    own_later, *_ = lax.optimization_barrier((hidden_rows[1], *arrived))
    near_later, far_later, _ = gather_near(own_later, -1)
    pieces = slot_gradient(0, place, row_counts, grad_t, near)
    pieces, far = lax.optimization_barrier((pieces, far))
    pieces = slot_gradient(0, place, row_counts, grad_t, gather_far(far), pieces)
    pieces, _ = lax.optimization_barrier((pieces, near_later[1][1][1][2]))
    received_first = exchange(pieces)
    columns = near_later + gather_far_apart(far_later, near_later[2][1][1][2])
    received_second = exchange(slot_gradient(1, place, row_counts, grad_t, columns))
    owner_pieces = sum_copies(replicas, owner_map, received_first, received_second)
    gradient = exchange(owner_pieces)
    state = (gradient, master, first_moment, second_moment)
    weight_pieces = adam_update(weights_kernel, "new_weights", None, *state)
    updated, new_first, new_second = adam_update(
        state_kernel, "new_state", (jnp.float32, jnp.bfloat16, jnp.bfloat16), *state
    )
    copies = spread_copies(next_replicas, owner_map, exchange(weight_pieces))
    next_copies = order_pieces(exchange(copies))
    return (updated, new_first, new_second, next_copies)


def solution(mesh):
    placed = (
        P("ep", None, "dp"),
        P("ep", None, "dp"),
        P("ep"),
        P(),
        P(),
        P(),
        P("ep", "dp", None),
        P("ep", "dp", None),
        P("ep", "dp", None),
    )
    return jax.shard_map(
        shards,
        mesh=mesh,
        in_specs=placed,
        out_specs=(
            P("ep", "dp", None),
            P("ep", "dp", None),
            P("ep", "dp", None),
            P("ep", "dp", None),
        ),
        check_vma=False,
    )
```

```python
import functools
import itertools

import jax
import jax.numpy as jnp
from jax import lax
from jax.experimental import pallas as pl
from jax.experimental.pallas import tpu as pltpu
from jax.sharding import PartitionSpec as P

beta_first = 0.9
beta_second = 0.95
learn_rate = 0.001
adam_epsilon = 1e-08

ROW_CUTS = 4
COL_CUTS = 8
LEAD = 1
PIECE = 112
LANES = 128
VMEM = 48 * 1024 * 1024
VMEM_FAR = 48 * 1024 * 1024
VMEM_LOW = 16 * 1024 * 1024
VMEM_ALL = 62 * 1024 * 1024


def any_spec():
    return pl.BlockSpec(memory_space=pl.ANY)


def smem_spec():
    return pl.BlockSpec(memory_space=pltpu.SMEM)


def grad_kernel(slot, columns, place_ref, counts_ref, grad_ref, *refs):
    taken = sum(choices for _, parts in columns for *_, choices in parts)
    part_refs = refs[:taken]
    out_ref, grad_v, hidden_v, grad_sem, hidden_sems = refs[-5:]
    rows = grad_v.shape[1]
    load_grad = pltpu.make_async_copy(grad_ref.at[slot], grad_v, grad_sem)
    load_grad.start()
    core_here = lax.rem(place_ref[0], 2)
    loads = []
    at = 0
    for i, (_, parts) in enumerate(columns):
        for core, start, size, choices in parts:
            into = hidden_v.at[i, pl.ds(start, size), pl.ds(core * LANES, LANES)]
            choice = [
                pltpu.make_async_copy(part_refs[at + k], into, hidden_sems.at[at]) for k in range(choices)
            ]
            if choices == 1:
                choice[0].start()
            else:
                pl.when(core_here == LEAD)(choice[0].start)
                pl.when(core_here != LEAD)(choice[1].start)
            loads.append((i, choice[0]))
            at += choices
    load_grad.wait()
    live = lax.broadcasted_iota(jnp.int32, (PIECE, rows), 1) < counts_ref[slot]
    for r in range(ROW_CUTS):
        cut = grad_v[pl.ds(r * PIECE, PIECE), :]
        grad_v[pl.ds(r * PIECE, PIECE), :] = jnp.where(live, cut, jnp.zeros_like(cut))
    x_here = place_ref[0] // 2
    for _, load in loads:
        load.wait()

    @pl.loop(0, len(columns))
    def _(i):
        step = sum(jnp.where(i == k, there, 0) for k, (there, _) in enumerate(columns))
        product = jnp.dot(grad_v[...], hidden_v[i], preferred_element_type=jnp.float32)
        product = product.astype(out_ref.dtype)
        x_there = lax.rem(x_here + step, COL_CUTS // 2)
        for c in range(2):
            column = 2 * x_there + (core_here if c == 0 else 1 - core_here)
            for r in range(ROW_CUTS):
                out_ref[r * COL_CUTS + column] = product[
                    r * PIECE : (r + 1) * PIECE, c * LANES : (c + 1) * LANES
                ]


def grad_far_kernel(slot, columns, place_ref, counts_ref, grad_ref, *refs):
    *inner, near_ref, out_ref, stage, grad_v, hidden_v, grad_sem, hidden_sems, out_sems = refs
    del near_ref
    grad_kernel(
        slot, columns, place_ref, counts_ref, grad_ref, *inner, stage, grad_v, hidden_v, grad_sem, hidden_sems
    )
    x_there = lax.rem(place_ref[0] // 2 + columns[0][0], COL_CUTS // 2)
    stores = []
    for r in range(ROW_CUTS):
        pair = pl.ds(r * COL_CUTS + 2 * x_there, 2)
        stores.append(pltpu.make_async_copy(stage.at[pair], out_ref.at[pair], out_sems.at[r]))
    for store in stores:
        store.start()
    for store in stores:
        store.wait()


def slot_gradient(slot, place, counts, grad_t, columns, near=None):
    rows = grad_t.shape[2]
    width = grad_t.shape[1]
    parts = [part for _, shard in columns for _, _, *choices in shard for part in choices]
    plan = tuple(
        (step, tuple((core, start, part[0].shape[0], len(part)) for core, start, *part in shard))
        for step, shard in columns
    )
    piece_shape = (ROW_CUTS * COL_CUTS, PIECE, LANES)
    scratch = [
        pltpu.VMEM((width, rows), jnp.bfloat16),
        pltpu.VMEM((len(plan), rows, 2 * LANES), jnp.bfloat16),
        pltpu.SemaphoreType.DMA,
        pltpu.SemaphoreType.DMA((len(parts),)),
    ]
    specs = [smem_spec(), smem_spec()] + [any_spec()] * (1 + len(parts))
    cost = pl.CostEstimate(
        flops=2 * width * rows * 256 * len(plan), bytes_accessed=(2_000_000 + 38_000_000 * slot) * len(plan), transcendentals=0
    )
    if near is None:
        return pl.pallas_call(
            functools.partial(grad_kernel, slot, plan),
            out_shape=jax.ShapeDtypeStruct(piece_shape, jnp.bfloat16),
            in_specs=specs,
            out_specs=pl.BlockSpec(memory_space=pltpu.VMEM),
            scratch_shapes=scratch,
            compiler_params=pltpu.CompilerParams(vmem_limit_bytes=VMEM),
            cost_estimate=cost,
            name="gradient_near",
        )(place, counts, grad_t, *parts)
    return pl.pallas_call(
        functools.partial(grad_far_kernel, slot, plan),
        out_shape=jax.ShapeDtypeStruct(piece_shape, jnp.bfloat16),
        in_specs=specs + [any_spec()],
        out_specs=any_spec(),
        scratch_shapes=[pltpu.VMEM(piece_shape, jnp.bfloat16)]
        + scratch
        + [pltpu.SemaphoreType.DMA((ROW_CUTS,))],
        input_output_aliases={3 + len(parts): 0},
        compiler_params=pltpu.CompilerParams(vmem_limit_bytes=VMEM_FAR),
        cost_estimate=cost,
        name="gradient_far",
    )(place, counts, grad_t, *parts, near)


def list_length(lists_ref, e):
    length = jnp.int32(0)
    for j in range(lists_ref.shape[1]):
        length = length + (lists_ref[e, j] >= 0).astype(jnp.int32)
    return length


def sum_kernel(replicas_ref, owners_ref, first_ref, second_ref, out_ref, held, sems):
    loads = [
        pltpu.make_async_copy(src, held.at[s], sems.at[s])
        for s, src in enumerate((first_ref, second_ref))
    ]
    for load in loads:
        load.start()
    for load in loads:
        load.wait()

    @pl.loop(0, replicas_ref.shape[0])
    def _(e):
        def take(j):
            g = replicas_ref[e, j]
            return held[lax.rem(g, 2), g // 2].astype(jnp.float32)

        total = lax.fori_loop(
            1, list_length(replicas_ref, e), lambda j, total: total + take(j), take(0)
        )
        out_ref[owners_ref[e]] = total.astype(out_ref.dtype)


def sum_copies(replicas, owner_map, first, second):
    pieces = first.shape[0]
    return pl.pallas_call(
        sum_kernel,
        out_shape=jax.ShapeDtypeStruct((pieces, PIECE, LANES), jnp.bfloat16),
        in_specs=[smem_spec(), smem_spec(), any_spec(), any_spec()],
        out_specs=pl.BlockSpec(memory_space=pltpu.VMEM),
        scratch_shapes=[
            pltpu.VMEM((2, pieces, PIECE, LANES), jnp.bfloat16),
            pltpu.SemaphoreType.DMA((2,)),
        ],
        compiler_params=pltpu.CompilerParams(vmem_limit_bytes=VMEM),
        name="sum_copies",
    )(replicas, owner_map, first, second)


def adam_cut(r, c, grad_ref, master_ref, first_ref, second_ref):
    cut = (0, pl.ds(r * PIECE, PIECE), pl.ds(c * LANES, LANES))
    gradient = grad_ref[r * COL_CUTS + c].astype(jnp.float32)
    first_new = beta_first * first_ref[cut].astype(jnp.float32) + (1.0 - beta_first) * gradient
    second_new = (
        beta_second * second_ref[cut].astype(jnp.float32) + (1.0 - beta_second) * gradient * gradient
    )
    updated = master_ref[cut] - learn_rate * first_new / (jnp.sqrt(second_new) + adam_epsilon)
    return cut, first_new, second_new, updated


def weights_kernel(grad_ref, master_ref, first_ref, second_ref, sent_ref):
    for r, c in itertools.product(range(2), range(COL_CUTS)):
        _, _, _, updated = adam_cut(r, c, grad_ref, master_ref, first_ref, second_ref)
        sent_ref[r * COL_CUTS + c] = updated.astype(sent_ref.dtype)


def state_kernel(grad_ref, master_ref, first_ref, second_ref, master_out, first_out, second_out):
    for r, c in itertools.product(range(2), range(COL_CUTS)):
        cut, first_new, second_new, updated = adam_cut(r, c, grad_ref, master_ref, first_ref, second_ref)
        master_out[cut] = updated
        first_out[cut] = first_new.astype(first_out.dtype)
        second_out[cut] = second_new.astype(second_out.dtype)


def adam_update(kernel, name, kinds, gradient, master, first_moment, second_moment):
    rows = pl.BlockSpec((1, 2 * PIECE, COL_CUTS * LANES), lambda r: (0, r, 0))
    pieces = pl.BlockSpec((2 * COL_CUTS, PIECE, LANES), lambda r: (r, 0, 0))
    if kinds is None:
        shapes = jax.ShapeDtypeStruct(gradient.shape, jnp.bfloat16)
        out_specs = pieces
    else:
        shapes = tuple(jax.ShapeDtypeStruct(master.shape, kind) for kind in kinds)
        out_specs = (rows,) * len(kinds)
    return pl.pallas_call(
        kernel,
        grid=(ROW_CUTS // 2,),
        out_shape=shapes,
        in_specs=[pieces, rows, rows, rows],
        out_specs=out_specs,
        compiler_params=pltpu.CompilerParams(vmem_limit_bytes=VMEM if kinds is None else VMEM_LOW),
        cost_estimate=pl.CostEstimate(flops=8_000_000, bytes_accessed=9_000_000, transcendentals=0),
        name=name,
    )(gradient, master, first_moment, second_moment)


def spread_kernel(lists_ref, owners_ref, weights_ref, out_ref, sem):
    @pl.loop(0, lists_ref.shape[0])
    def _(e):
        weights = weights_ref.at[owners_ref[e]]

        def put(j, carry):
            g = lists_ref[e, j]
            pltpu.make_async_copy(weights, out_ref.at[g // 2, lax.rem(g, 2)], sem).start()
            return carry

        lax.fori_loop(0, list_length(lists_ref, e), put, 0)

    pltpu.make_async_copy(out_ref, out_ref, sem).wait()


def spread_copies(next_replicas, owner_map, weights):
    pieces = weights.shape[0]
    return pl.pallas_call(
        spread_kernel,
        out_shape=jax.ShapeDtypeStruct((pieces, 2, PIECE, LANES), jnp.bfloat16),
        in_specs=[smem_spec(), smem_spec(), pl.BlockSpec(memory_space=pltpu.VMEM)],
        out_specs=any_spec(),
        scratch_shapes=[pltpu.SemaphoreType.DMA],
        compiler_params=pltpu.CompilerParams(vmem_limit_bytes=VMEM_ALL),
        name="spread_copies",
    )(next_replicas, owner_map, weights)


def order_kernel(pieces_ref, out_ref, ordered, load_sems, store_sems):
    loads = [
        [
            pltpu.make_async_copy(
                pieces_ref.at[r, c], ordered.at[:, r, :, pl.ds(c * LANES, LANES)], load_sems.at[r, c]
            )
            for c in range(COL_CUTS)
        ]
        for r in range(ROW_CUTS)
    ]
    for row in loads:
        for load in row:
            load.start()
    stores = []
    for r, row in enumerate(loads):
        for load in row:
            load.wait()
        store = pltpu.make_async_copy(ordered.at[:, r], out_ref.at[:, r], store_sems.at[r])
        store.start()
        stores.append(store)
    for store in stores:
        store.wait()


def order_pieces(pieces):
    shape = (2, ROW_CUTS, PIECE, COL_CUTS * LANES)
    return pl.pallas_call(
        order_kernel,
        out_shape=jax.ShapeDtypeStruct(shape, jnp.bfloat16),
        in_specs=[any_spec()],
        out_specs=any_spec(),
        scratch_shapes=[
            pltpu.VMEM(shape, jnp.bfloat16),
            pltpu.SemaphoreType.DMA((ROW_CUTS, COL_CUTS)),
            pltpu.SemaphoreType.DMA((ROW_CUTS,)),
        ],
        compiler_params=pltpu.CompilerParams(vmem_limit_bytes=VMEM_LOW),
        name="order_pieces",
    )(pieces.reshape(ROW_CUTS, COL_CUTS, 2, PIECE, LANES)).reshape(2, ROW_CUTS * PIECE, COL_CUTS * LANES)


def x_shift(array, step, cores=(0, 1)):
    pairs = [(2 * x + c, 2 * ((x + step) % 4) + c) for x in range(4) for c in cores]
    return lax.ppermute(array, "dp", pairs)


def core_swap(array):
    pairs = [(2 * x + c, 2 * x + 1 - c) for x in range(4) for c in range(2)]
    return lax.ppermute(array, "dp", pairs)


def gather_near(own, way):
    ahead = x_shift(own, -1)
    behind = x_shift(own, 1)
    far = x_shift(behind if way > 0 else ahead, way)
    near = [
        (step, [(0, 0, shard), (1, 0, core_swap(shard))])
        for step, shard in ((0, own), (1, ahead), (3, behind))
    ]
    return near, far, (ahead, behind)


def gather_far(far):
    return [(2, [(0, 0, far), (1, 0, core_swap(far))])]


def gather_far_apart(far, behind_swapped):
    to_lead = lax.ppermute(far, "dp", [(2 * x + 1 - LEAD, 2 * x + LEAD) for x in range(4)])
    return [(2, [(0, 0, far), (1, 0, to_lead, x_shift(behind_swapped, 1, (1 - LEAD,)))])]


def exchange(pieces):
    return lax.all_to_all(pieces, "ep", split_axis=0, concat_axis=0, tiled=True)


def shards(
    hidden_rows,
    out_grad,
    row_counts,
    replicas,
    next_replicas,
    owner_map,
    master,
    first_moment,
    second_moment,
):
    place = lax.axis_index("dp").reshape(1).astype(jnp.int32)
    grad_t = jnp.swapaxes(out_grad, 1, 2)
    near, far, arrived = gather_near(hidden_rows[0], 1)
    own_later, *_ = lax.optimization_barrier((hidden_rows[1], *arrived))
    near_later, far_later, _ = gather_near(own_later, -1)
    pieces = slot_gradient(0, place, row_counts, grad_t, near)
    pieces, far = lax.optimization_barrier((pieces, far))
    pieces = slot_gradient(0, place, row_counts, grad_t, gather_far(far), pieces)
    pieces, _ = lax.optimization_barrier((pieces, near_later[1][1][1][2]))
    received_first = exchange(pieces)
    columns = near_later + gather_far_apart(far_later, near_later[2][1][1][2])
    received_second = exchange(slot_gradient(1, place, row_counts, grad_t, columns))
    owner_pieces = sum_copies(replicas, owner_map, received_first, received_second)
    gradient = exchange(owner_pieces)
    state = (gradient, master, first_moment, second_moment)
    weight_pieces = adam_update(weights_kernel, "new_weights", None, *state)
    updated, new_first, new_second = adam_update(
        state_kernel, "new_state", (jnp.float32, jnp.bfloat16, jnp.bfloat16), *state
    )
    copies = spread_copies(next_replicas, owner_map, exchange(weight_pieces))
    next_copies = order_pieces(exchange(copies))
    return (updated, new_first, new_second, next_copies)


def solution(mesh):
    placed = (
        P("ep", None, "dp"),
        P("ep", None, "dp"),
        P("ep"),
        P(),
        P(),
        P(),
        P("ep", "dp", None),
        P("ep", "dp", None),
        P("ep", "dp", None),
    )
    return jax.shard_map(
        shards,
        mesh=mesh,
        in_specs=placed,
        out_specs=(
            P("ep", "dp", None),
            P("ep", "dp", None),
            P("ep", "dp", None),
            P("ep", "dp", None),
        ),
        check_vma=False,
    )
```
